512 devices in a mesh: section: 32 (over x, z), replica: 16 (over y, core).
Axes of the slice: x: 4, y: 8, z: 8, core: 2. Of those that a mesh axis runs over, the one named last changes fastest.
Arguments:
- hidden_in: bfloat16 [128, 8192], P('replica'), may hold values from -6 to 6
- norm_gain: float32 [32, 8192], P('section'), may hold values from 0.5 to 2
- new_kv: bfloat16 [32, 128, 2, 4, 128], P('section', 'replica'), may hold values from -6 to 6
- parked: bfloat16 [32, 256, 2, 4, 128, 128], P('section', 'replica'), may hold values from -6 to 6
- cache_len: int32 [128], P('replica'), may hold values from 1 to 256
- block_home: int32 [128, 2], P('replica'), may hold values from 0 to 255, as said below
Outputs:
- section_outputs: bfloat16 [32, 128, 8192], P('section', 'replica')
The draws below stay inside these ranges and needn't reach their ends.
Inputs may be any that keep to these rules, and one draw needn't show every extreme that they name: `block_home`: every parked block is named exactly once. Parked block b lies on replica b // 16. The rows of replica r name exactly 2 blocks lying on each of replicas r + 8, r + 16 // 2 + 1, ..., r + 16 - 1 (counted cyclically) and none on the others.
All inputs are finite; a program needn't handle non-finite values.
Results may differ from the reference program's by a relative error of at most 0.035.
Values may be sent and summed in bfloat16 or wider, within the bound.
A program may use at most 64 MiB of HBM per device.

```python
import math
import jax
import jax.numpy as jnp
from jax import lax

HQ = 64
KVH = 4
HD = 128
BLK = 128
NB = 2
ROWS = 8
ACT = 8192
PARK = 16
SEQS = 128
N_SECTION = 32
N_REPLICA = 16


def draw_block_home(key, part):
    key = jax.random.fold_in(key, 11)
    count = ROWS * NB
    half = N_REPLICA // 2
    cap = count // half
    key_slots, key_local = jax.random.split(key, 2)
    slot_perm = jax.vmap(lambda k: jax.random.permutation(k, count))(jax.random.split(key_slots, N_REPLICA))
    local_perm = jax.vmap(lambda k: jax.random.permutation(k, count))(jax.random.split(key_local, N_REPLICA))
    offset = slot_perm // cap
    within = slot_perm % cap
    source = (jnp.arange(N_REPLICA, dtype=jnp.int32)[:, None] + half + offset) % N_REPLICA
    local = local_perm[source, offset * cap + within]
    ids = source * count + local
    return ids.reshape(N_REPLICA * ROWS, NB).astype(jnp.int32)


def touch_ends(result, rng, low, high):
    place = [jax.random.randint(jax.random.fold_in(rng, axis), (), 0, length) for axis, length in enumerate(result.shape)]
    main_axis = result.shape.index(max(result.shape))
    beside = place[:main_axis] + [(place[main_axis] + 1) % result.shape[main_axis]] + place[main_axis + 1:]
    return result.at[tuple(place)].set(low).at[tuple(beside)].set(high)


def level_of(key, dims, shards, least, high):
    def one(dim, parts):
        draws = jax.random.uniform(jax.random.fold_in(jax.random.fold_in(key, 6), dim), (parts,), jnp.float32, least / len(shards), high / len(shards))
        return jnp.repeat(jnp.exp(draws), dims[dim] // parts).reshape((-1,) + (1,) * (len(dims) - dim - 1))

    level = one(*shards[0])
    for cut in shards[1:]:
        level = level * one(*cut)
    return level


def bell_draw(rng, shape, width, bound, cuts=(), held_as=jnp.bfloat16):
    result = jax.random.normal(rng, shape, jnp.float32) * width
    if len(cuts) > 0:
        result = level_of(rng, shape, cuts, -0.22, 0.18) * result
    return jnp.clip(result, min=-bound, max=bound).astype(held_as)


def setup_inputs(seed: int = 0) -> dict:
    seeds = jax.random.split(jax.random.key(seed), 7)
    return {
        "hidden_in": bell_draw(seeds[0], (SEQS, ACT), 1.0, 6.0, ((0, 16),)),
        "norm_gain": jnp.clip(jnp.exp(math.log(2.0) - 1.3862944 * jax.random.uniform(seeds[1], (N_SECTION, ACT), jnp.float32) ** level_of(seeds[1], (N_SECTION, ACT), ((0, 32),), -0.2, 0.2)), 0.5, 2.0),
        "new_kv": bell_draw(seeds[2], (N_SECTION, SEQS, 2, KVH, HD), 1.0, 6.0, ((0, 32), (1, 16))),
        "parked": bell_draw(seeds[3], (N_SECTION, N_REPLICA * PARK, 2, KVH, BLK, HD), 1.0, 6.0, ((0, 32), (1, 16))),
        "cache_len": touch_ends(jax.random.randint(seeds[4], (SEQS,), 1, NB * BLK + 1), jax.random.fold_in(seeds[4], 1), 1, NB * BLK).astype(jnp.int32),
        "block_home": draw_block_home(jax.random.fold_in(seeds[6], 71), 0),
    }


def layer_rows(x, gain, cache, new_kv, lens):
    rows = x.shape[0]
    group = HQ // KVH
    xf = x.astype(jnp.float32)
    normed = xf * lax.rsqrt(lax.optimization_barrier(jnp.mean(xf * xf, axis=-1, keepdims=True)) + 1e-05) * gain
    q = normed.astype(jnp.bfloat16).reshape(rows, KVH, group, HD).astype(jnp.float32)
    keys = cache[:, :, 0].astype(jnp.float32)
    vals = cache[:, :, 1].astype(jnp.float32)
    scale = 1.0 / HD ** 0.5
    scores = jnp.einsum('rkgd,rnktd->rkgnt', q, keys) * scale
    pos = jnp.arange(NB * BLK, dtype=jnp.int32).reshape(NB, BLK)
    valid = pos[None, :, :] < lens[:, None, None]
    scores = jnp.where(valid[:, None, None, :, :], scores, -1e+30)
    new_score = jnp.einsum('rkgd,rkd->rkg', q, new_kv[:, 0].astype(jnp.float32)) * scale
    top = jnp.maximum(lax.optimization_barrier(jnp.max(scores, axis=(3, 4))), new_score)
    expo = jnp.exp(scores - top[..., None, None])
    expo_new = jnp.exp(new_score - top)
    total = lax.optimization_barrier(jnp.sum(expo, axis=(3, 4))) + expo_new
    weights = (expo / total[..., None, None]).astype(jnp.bfloat16).astype(jnp.float32)
    weight_new = (expo_new / total).astype(jnp.bfloat16).astype(jnp.float32)
    attended = jnp.einsum('rkgnt,rnktd->rkgd', weights, vals)
    attended = attended + weight_new[..., None] * new_kv[:, 1].astype(jnp.float32)[:, :, None, :]
    return (xf + attended.reshape(rows, HQ * HD)).astype(jnp.bfloat16)

def reference(hidden_in, norm_gain, new_kv, parked, cache_len, block_home):

    def one_section(x, pieces):
        gain, kv_new, blocks = pieces
        cache = jnp.take(blocks, block_home.reshape(-1), axis=0)
        cache = cache.reshape(x.shape[0], NB, 2, KVH, BLK, HD)
        y = layer_rows(x, gain, cache, kv_new, cache_len)
        return (y, y)
    final, outs = lax.scan(one_section, hidden_in, (norm_gain, new_kv, parked))
    return outs
```

```python
import functools
import math

import jax
import jax.numpy as jnp
from jax import lax
from jax.experimental import pallas as pl
from jax.experimental.pallas import tpu as pltpu
from jax.sharding import PartitionSpec as P

HQ = 64
KVH = 4
HD = 128
BLK = 128
NB = 2
GROUP = HQ // KVH
HALF = 8
MID = 4
STEP = 1
MESH = pl.DeviceIdType.MESH


def dot_t(a, b):
    return lax.dot_general(a, b, (((1,), (1,)), ((), ())), preferred_element_type=jnp.float32)


def dot(a, b):
    return jnp.dot(a, b, preferred_element_type=jnp.float32)


def layer_row(x, gain, kv, slots, length, new):
    xf = x.astype(jnp.float32)
    q = (xf * gain).astype(jnp.bfloat16)
    square = jnp.sum(jnp.sum(xf * xf, axis=0, keepdims=True), axis=1, keepdims=True)
    factor = lax.rsqrt(square * (1.0 / (HQ * HD)) + 1e-05) * (math.log2(math.e) / HD**0.5)
    pos = lax.broadcasted_iota(jnp.int32, (1, NB * BLK), 1)
    bias = jnp.where(pos < length, 0.0, -1e30)
    scores = []
    news = []
    for h in range(KVH):
        qh = q[h * GROUP : (h + 1) * GROUP]
        parts = [dot_t(qh, kv[slots[j], 0, h]) for j in range(NB)]
        scores.append(jnp.concatenate(parts, axis=1))
        news.append(
            jnp.sum(qh.astype(jnp.float32) * new[h : h + 1], axis=1, keepdims=True)
        )
    score = jnp.concatenate(scores, axis=0) + bias
    score_new = jnp.concatenate(news, axis=0)
    top = jnp.maximum(jnp.max(score, axis=1, keepdims=True), score_new)
    expo = jnp.exp2((score - top) * factor)
    expo_new = jnp.exp2((score_new - top) * factor)
    total = jnp.sum(expo, axis=1, keepdims=True) + expo_new
    weights = expo.astype(jnp.bfloat16)
    outs = []
    for h in range(KVH):
        rows = slice(h * GROUP, (h + 1) * GROUP)
        part = expo_new[rows] * new[KVH + h : KVH + h + 1]
        for j in range(NB):
            part = part + dot(weights[rows, j * BLK : (j + 1) * BLK], kv[slots[j], 1, h])
        outs.append(part)
    attended = jnp.concatenate(outs, axis=0) / total
    return (xf + attended).astype(jnp.bfloat16)


def kernel(
    sections, replicas, rows,
    meta_ref, hidden_ref, new_ref, gain_ref, parked_ref, out_ref,
    park, send, kv, metav, metas, x_in, x_out, new_in, new_f,
    park_sem, smem_sem, meta_send, meta_recv, kv_send, kv_recv,
    x_send, x_recv, out_send, out_recv, first_send, new_send, new_recv,
):
    s = lax.axis_index("section")
    p = lax.axis_index("replica")
    turns = rows // STEP

    def at(shift):
        return {"replica": lax.rem(p + shift + 2 * replicas, replicas)}

    park_copy = pltpu.make_async_copy(parked_ref, park, park_sem)
    park_copy.start()

    barrier = pltpu.get_barrier_semaphore()

    @pl.loop(1, replicas)
    def _(j):
        pl.semaphore_signal(barrier, inc=1, device_id=at(j), device_id_type=MESH)

    @pl.when(s > 0)
    def _():
        pl.semaphore_signal(barrier, inc=1, device_id={"section": s - 1}, device_id_type=MESH)

    pl.semaphore_wait(barrier, replicas - 1 + (s < sections - 1).astype(jnp.int32))

    def meta_copy(k):
        return pltpu.make_async_remote_copy(
            meta_ref, metav.at[k], meta_send.at[k], meta_recv.at[k],
            device_id=at(HALF + k), device_id_type=MESH,
        )

    def hidden_copy(m):
        return pltpu.make_async_remote_copy(
            hidden_ref.at[pl.ds(m * STEP, STEP)], x_in.at[pl.ds(m * STEP, STEP)],
            first_send.at[m], x_recv.at[m],
            device_id=at(HALF + MID), device_id_type=MESH,
        )

    new_copy = pltpu.make_async_remote_copy(
        new_ref, new_in, new_send, new_recv, device_id=at(HALF + MID), device_id_type=MESH
    )

    @pl.loop(0, HALF)
    def _(k):
        meta_copy(k).start()

    new_copy.start()

    @pl.when(s == 0)
    def _():
        @pl.loop(0, turns)
        def _(m):
            hidden_copy(m).start()

    @pl.loop(0, HALF)
    def _(k):
        meta_copy(k).wait_recv()

    to_smem = pltpu.make_async_copy(metav, metas, smem_sem)
    to_smem.start()
    to_smem.wait()
    park_copy.wait()

    def kv_copy(k):
        return pltpu.make_async_remote_copy(
            send.at[pl.ds(NB * k, NB)], kv.at[pl.ds(NB * k, NB)],
            kv_send.at[k], kv_recv.at[k],
            device_id=at(MID - k), device_id_type=MESH,
        )

    def pick(k, dst):
        for j in range(NB):
            block = metas[k, 0, NB * k + j]
            for half in range(2):
                for h in range(KVH):
                    dst[NB * k + j, half, h] = park[block, half, h]

    @pl.loop(0, HALF - 1)
    def _(t):
        k = t + t // MID
        pick(k, send)
        kv_copy(k).start()

    pick(MID, kv)

    new_copy.wait_recv()
    new_f[...] = new_in[...].astype(jnp.float32).reshape(new_f.shape)
    gain = gain_ref[...]

    @pl.loop(0, HALF - 1)
    def _(t):
        kv_copy(t + t // MID).wait_recv()

    def relay_copy(m):
        return pltpu.make_async_remote_copy(
            x_out.at[pl.ds(m * STEP, STEP)], x_in.at[pl.ds(m * STEP, STEP)],
            x_send.at[m], x_recv.at[m],
            device_id={"section": s + 1}, device_id_type=MESH,
        )

    def home_copy(m):
        return pltpu.make_async_remote_copy(
            x_out.at[pl.ds(m * STEP, STEP)], out_ref.at[pl.ds(m * STEP, STEP)],
            out_send.at[m], out_recv.at[m],
            device_id=at(-HALF - MID), device_id_type=MESH,
        )

    @pl.loop(0, turns)
    def _(m):
        hidden_copy(m).wait_recv()
        for i in range(STEP):
            row = m * STEP + i
            slots = [metas[MID, 1, NB * row + j] for j in range(NB)]
            length = metas[MID, 2, row]
            x_out[row] = layer_row(x_in[row], gain, kv, slots, length, new_f[row])

        @pl.when(s < sections - 1)
        def _():
            relay_copy(m).start()

        home_copy(m).start()

    @pl.loop(0, HALF)
    def _(k):
        meta_copy(k).wait_send()

    @pl.loop(0, HALF - 1)
    def _(t):
        kv_copy(t + t // MID).wait_send()

    new_copy.wait_send()

    @pl.when(s == 0)
    def _():
        @pl.loop(0, turns)
        def _(m):
            hidden_copy(m).wait_send()

    @pl.loop(0, turns)
    def _(m):
        @pl.when(s < sections - 1)
        def _():
            relay_copy(m).wait_send()

        home_copy(m).wait_send()
        home_copy(m).wait_recv()


def per_device(hidden_in, norm_gain, new_kv, parked, cache_len, block_home):
    replicas = lax.axis_size("replica")
    sections = lax.axis_size("section")
    me = lax.axis_index("replica")
    blocks = parked[0]
    park_count = blocks.shape[0]
    rows = block_home.shape[0]
    count = rows * NB

    flat = block_home.reshape(count)
    near = lax.rem(flat - (me + HALF) * park_count + 2 * replicas * park_count, replicas * park_count)
    place = jnp.sum((near[None, :] < near[:, None]).astype(jnp.int32), axis=1)
    hit = place[None, :] == jnp.arange(count, dtype=jnp.int32)[:, None]
    local = jnp.sum(jnp.where(hit, lax.rem(flat, park_count)[None, :], 0), axis=1)
    meta = jnp.stack([
        jnp.pad(local, (0, 128 - count)),
        jnp.pad(place, (0, 128 - count)),
        jnp.pad(cache_len, (0, 128 - rows)),
    ])
    meta = jnp.pad(meta, ((0, 5), (0, 0)))

    turns = rows // STEP
    vmem = pl.BlockSpec(memory_space=pltpu.VMEM)
    hbm = pl.BlockSpec(memory_space=pl.ANY)
    dma = pltpu.SemaphoreType.DMA
    out = pl.pallas_call(
        functools.partial(kernel, sections, replicas, rows),
        out_shape=jax.ShapeDtypeStruct((rows, HQ, HD), jnp.bfloat16),
        in_specs=[vmem, vmem, vmem, vmem, hbm],
        out_specs=hbm,
        scratch_shapes=[
            pltpu.VMEM(blocks.shape, jnp.bfloat16),
            pltpu.VMEM(blocks.shape, jnp.bfloat16),
            pltpu.VMEM(blocks.shape, jnp.bfloat16),
            pltpu.VMEM((HALF, 8, 128), jnp.int32),
            pltpu.SMEM((HALF, 8, 128), jnp.int32),
            pltpu.VMEM((rows, HQ, HD), jnp.bfloat16),
            pltpu.VMEM((rows, HQ, HD), jnp.bfloat16),
            pltpu.VMEM((rows * 2 * KVH, HD), jnp.bfloat16),
            pltpu.VMEM((rows, 2 * KVH, HD), jnp.float32),
            dma, dma,
            dma((HALF,)), dma((HALF,)), dma((HALF,)), dma((HALF,)),
            dma((turns,)), dma((turns,)), dma((turns,)), dma((turns,)), dma((turns,)),
            dma, dma,
        ],
        compiler_params=pltpu.CompilerParams(
            collective_id=0, has_side_effects=True, vmem_limit_bytes=32 * 1024 * 1024
        ),
    )(
        meta,
        hidden_in.reshape(rows, HQ, HD),
        new_kv[0].reshape(rows * 2 * KVH, HD),
        norm_gain.reshape(HQ, HD),
        blocks,
    )
    return out.reshape(1, rows, HQ * HD)


def solution(mesh):
    return jax.shard_map(
        per_device,
        mesh=mesh,
        in_specs=(
            P("replica", None),
            P("section", None),
            P("section", "replica", None, None, None),
            P("section", "replica", None, None, None, None),
            P("replica"),
            P("replica", None),
        ),
        out_specs=P("section", "replica", None),
        check_vma=False,
    )
```

```python
import functools
import math

import jax
import jax.numpy as jnp
from jax import lax
from jax.experimental import pallas as pl
from jax.experimental.pallas import tpu as pltpu
from jax.sharding import PartitionSpec as P

HQ = 64
KVH = 4
HD = 128
BLK = 128
NB = 2
GROUP = HQ // KVH
HALF = 8
MID = 4
MESH = pl.DeviceIdType.MESH


def dot_t(a, b):
    return lax.dot_general(a, b, (((1,), (1,)), ((), ())), preferred_element_type=jnp.float32)


def dot(a, b):
    return jnp.dot(a, b, preferred_element_type=jnp.float32)


def layer_row(x, gain, kv, slots, length, new):
    xf = x.astype(jnp.float32)
    q = (xf * gain).astype(jnp.bfloat16)
    square = jnp.sum(jnp.sum(xf * xf, axis=0, keepdims=True), axis=1, keepdims=True)
    factor = lax.rsqrt(square * (1.0 / (HQ * HD)) + 1e-05) * (math.log2(math.e) / HD**0.5)
    heads = [slice(h * GROUP, (h + 1) * GROUP) for h in range(KVH)]
    pad = jnp.zeros((BLK - 2 * KVH, HD), jnp.float32)
    new_keys, new_values = [
        jnp.concatenate([new[i], pad], axis=0).astype(jnp.bfloat16) for i in range(2)
    ]
    pos = lax.broadcasted_iota(jnp.int32, (1, BLK), 1)
    own = lax.broadcasted_iota(jnp.int32, (HQ, BLK), 0) // GROUP
    masks = [pos + j * BLK < length for j in range(NB)]
    masks.append(lax.broadcasted_iota(jnp.int32, (HQ, BLK), 1) == own)
    cached = jnp.concatenate(
        [
            dot(q[rows], jnp.concatenate([kv[slots[j], 0, h] for j in range(NB)], axis=1))
            for h, rows in enumerate(heads)
        ],
        axis=0,
    )
    scores = [cached[:, j * BLK : (j + 1) * BLK] for j in range(NB)]
    scores.append(dot_t(q, new_keys))
    scores = [part + jnp.where(mask, 0.0, -1e30) for part, mask in zip(scores, masks)]
    top = jnp.max(functools.reduce(jnp.maximum, scores), axis=1, keepdims=True)
    expos = [jnp.exp2((part - top) * factor) for part in scores]
    total = jnp.sum(sum(expos), axis=1, keepdims=True)
    weights = [part.astype(jnp.bfloat16) for part in expos]
    cached = jnp.concatenate(weights[:NB], axis=1)
    attended = dot(weights[NB], new_values) + jnp.concatenate(
        [
            dot(cached[rows], jnp.concatenate([kv[slots[j], 1, h] for j in range(NB)], axis=0))
            for h, rows in enumerate(heads)
        ],
        axis=0,
    )
    return (xf + attended / total).astype(jnp.bfloat16)


def kernel(
    sections, replicas, rows,
    meta_ref, hidden_ref, new_ref, gain_ref, parked_ref, out_ref,
    park, send, kv, metav, metas, hidden, hidden_f, first, x_in, x_out,
    new_raw, new_own, new_in, gain,
    local_sem, meta_send, meta_recv, kv_send, kv_recv,
    x_send, x_recv, out_send, out_recv, first_send, new_send, new_recv,
):
    s = lax.axis_index("section")
    p = lax.axis_index("replica")
    core = lax.rem(p, 2)
    worker = core == 1
    total = 2 * rows

    def at(shift):
        return {"replica": lax.rem(p + shift + 2 * replicas, replicas)}

    def local(i, src, dst):
        return pltpu.make_async_copy(src, dst, local_sem.at[i])

    fetch = [
        local(0, parked_ref, park),
        local(1, hidden_ref, hidden),
        local(2, new_ref, new_raw),
        local(3, gain_ref, gain),
    ]
    for copy in fetch:
        copy.start()

    barrier = pltpu.get_barrier_semaphore()

    @pl.loop(1, replicas)
    def _(j):
        pl.semaphore_signal(barrier, inc=1, device_id=at(j), device_id_type=MESH)

    @pl.when((s > 0) & worker)
    def _():
        pl.semaphore_signal(barrier, inc=1, device_id={"section": s - 1}, device_id_type=MESH)

    next_one = ((s < sections - 1) & worker).astype(jnp.int32)
    pl.semaphore_wait(barrier, replicas - 1 + next_one)

    def meta_copy(k):
        return pltpu.make_async_remote_copy(
            meta_ref, metav.at[k], meta_send.at[k], meta_recv.at[k],
            device_id=at(HALF + k), device_id_type=MESH,
        )

    mine = at(HALF + MID + 1 - core)

    def first_copy(m):
        return pltpu.make_async_remote_copy(
            first.at[m], x_in.at[core * rows + m], first_send.at[m], x_recv.at[core * rows + m],
            device_id=mine, device_id_type=MESH,
        )

    new_copy = pltpu.make_async_remote_copy(
        new_own, new_in.at[core], new_send, new_recv.at[core],
        device_id=mine, device_id_type=MESH,
    )

    @pl.loop(0, HALF)
    def _(k):
        meta_copy(k).start()

    @pl.loop(0, HALF)
    def _(k):
        meta_copy(k).wait_recv()

    to_smem = local(4, metav, metas)
    to_smem.start()
    to_smem.wait()
    fetch[0].wait()

    def target(k):
        to = p + MID - k + 2 * replicas
        return lax.rem(to - lax.rem(to, 2) + 1, replicas)

    def kv_pieces(k):
        home = lax.rem(p - k + 2 * replicas, 2)
        return (
            send.at[pl.ds(NB * k, NB)],
            kv.at[home, pl.ds(NB * k, NB)],
            kv_send.at[k],
            kv_recv.at[home, k],
        )

    def kv_copy(k):
        return pltpu.make_async_remote_copy(
            *kv_pieces(k), device_id={"replica": target(k)}, device_id_type=MESH
        )

    def kv_stay(k):
        src, dst, _, sem = kv_pieces(k)
        return pltpu.make_async_copy(src, dst, sem)

    @pl.loop(0, HALF)
    def _(k):
        for j in range(NB):
            block = metas[k, 0, NB * k + j]
            for h in range(KVH):
                send[NB * k + j, 0, h] = park[block, 0, h].T
                send[NB * k + j, 1, h] = park[block, 1, h]

        @pl.when(target(k) != p)
        def _():
            kv_copy(k).start()

        @pl.when(target(k) == p)
        def _():
            kv_stay(k).start()

    fetch[1].wait()
    fetch[2].wait()
    fetch[3].wait()

    @pl.loop(0, rows)
    def _(m):
        pair = new_raw[0, m].astype(jnp.float32)
        new_own[m, 0] = jnp.concatenate([pair[0], pair[1]], axis=0)
        new_own[m, 1] = jnp.concatenate([pair[1], pair[0]], axis=0)

    new_copy.start()

    @pl.when(s == 0)
    def _():
        for h in range(HQ):
            hidden_f[:, h, :] = hidden[:, h * HD : (h + 1) * HD].astype(jnp.float32)

        @pl.loop(0, rows)
        def _(m):
            first[m] = hidden_f[m].astype(jnp.bfloat16)
            first_copy(m).start()

    def arrival(home, k):
        return pltpu.make_async_remote_copy(
            send.at[pl.ds(0, NB)], kv.at[home, pl.ds(NB * k, NB)],
            kv_send.at[k], kv_recv.at[home, k],
            device_id={"replica": p}, device_id_type=MESH,
        )

    def row_arrival(i):
        return pltpu.make_async_remote_copy(
            x_out.at[i], x_in.at[i], x_send.at[i], x_recv.at[i],
            device_id={"section": s}, device_id_type=MESH,
        )

    def relay_copy(i):
        return pltpu.make_async_remote_copy(
            x_out.at[i], x_in.at[i], x_send.at[i], x_recv.at[i],
            device_id={"section": s + 1}, device_id_type=MESH,
        )

    def home_copy(i):
        home = i // rows
        return pltpu.make_async_remote_copy(
            x_out.at[i], out_ref.at[i - home * rows], out_send.at[i], out_recv.at[i - home * rows],
            device_id=at(MID - 1 + home), device_id_type=MESH,
        )

    @pl.when(worker)
    def _():
        for home in range(2):
            pltpu.make_async_remote_copy(
                new_own, new_in.at[home], new_send, new_recv.at[home],
                device_id={"replica": p}, device_id_type=MESH,
            ).wait_recv()

            @pl.loop(0, HALF)
            def _(k):
                arrival(home, k).wait_recv()

        @pl.loop(0, total)
        def _(i):
            home = i // rows
            row = i - home * rows
            info = MID + 1 - home
            row_arrival(i).wait_recv()
            slots = [metas[info, 1, j * rows + row] for j in range(NB)]
            length = metas[info, 2, row]
            x_out[i] = layer_row(
                x_in[i], gain[...], kv.at[home], slots, length, new_in[home, row]
            )

            @pl.when(s < sections - 1)
            def _():
                relay_copy(i).start()

            home_copy(i).start()

        @pl.loop(0, total)
        def _(i):
            @pl.when(s < sections - 1)
            def _():
                relay_copy(i).wait_send()

            home_copy(i).wait_send()

    @pl.loop(0, HALF)
    def _(k):
        meta_copy(k).wait_send()

        @pl.when(target(k) != p)
        def _():
            kv_copy(k).wait_send()

    new_copy.wait_send()

    @pl.loop(0, rows)
    def _(m):
        @pl.when(s == 0)
        def _():
            first_copy(m).wait_send()

        pltpu.make_async_remote_copy(
            x_out.at[m], out_ref.at[m], out_send.at[m], out_recv.at[m],
            device_id={"replica": p}, device_id_type=MESH,
        ).wait_recv()


def per_device(hidden_in, norm_gain, new_kv, parked, cache_len, block_home):
    replicas = lax.axis_size("replica")
    sections = lax.axis_size("section")
    me = lax.axis_index("replica")
    blocks = parked[0]
    park_count = blocks.shape[0]
    rows = block_home.shape[0]
    count = rows * NB

    flat = block_home.T.reshape(count)
    near = lax.rem(flat - (me + HALF) * park_count + 2 * replicas * park_count, replicas * park_count)
    place = jnp.sum((near[None, :] < near[:, None]).astype(jnp.int32), axis=1)
    hit = place[None, :] == jnp.arange(count, dtype=jnp.int32)[:, None]
    local = jnp.sum(jnp.where(hit, lax.rem(flat, park_count)[None, :], 0), axis=1)
    meta = jnp.stack([
        jnp.pad(local, (0, 128 - count)),
        jnp.pad(place, (0, 128 - count)),
        jnp.pad(cache_len, (0, 128 - rows)),
    ])
    meta = jnp.pad(meta, ((0, 5), (0, 0)))

    total = 2 * rows
    hbm = pl.BlockSpec(memory_space=pl.ANY)
    dma = pltpu.SemaphoreType.DMA
    out = pl.pallas_call(
        functools.partial(kernel, sections, replicas, rows),
        out_shape=jax.ShapeDtypeStruct((rows, HQ, HD), jnp.bfloat16),
        in_specs=[hbm] * 5,
        out_specs=hbm,
        scratch_shapes=[
            pltpu.VMEM(blocks.shape, jnp.bfloat16),
            pltpu.VMEM(blocks.shape, jnp.bfloat16),
            pltpu.VMEM((2,) + blocks.shape, jnp.bfloat16),
            pltpu.VMEM((HALF, 8, 128), jnp.int32),
            pltpu.SMEM((HALF, 8, 128), jnp.int32),
            pltpu.VMEM(hidden_in.shape, jnp.bfloat16),
            pltpu.VMEM((rows, HQ, HD), jnp.float32),
            pltpu.VMEM((rows, HQ, HD), jnp.bfloat16),
            pltpu.VMEM((total, HQ, HD), jnp.bfloat16),
            pltpu.VMEM((total, HQ, HD), jnp.bfloat16),
            pltpu.VMEM(new_kv.shape, jnp.bfloat16),
            pltpu.VMEM((rows, 2, 2 * KVH, HD), jnp.float32),
            pltpu.VMEM((2, rows, 2, 2 * KVH, HD), jnp.float32),
            pltpu.VMEM((HQ, HD), jnp.float32),
            dma((5,)),
            dma((HALF,)), dma((HALF,)), dma((HALF,)), dma((2, HALF)),
            dma((total,)), dma((total,)), dma((total,)), dma((rows,)),
            dma((rows,)), dma, dma((2,)),
        ],
        compiler_params=pltpu.CompilerParams(
            collective_id=0, has_side_effects=True, vmem_limit_bytes=56 * 1024 * 1024
        ),
    )(meta, hidden_in, new_kv, norm_gain.reshape(HQ, HD), blocks)
    return out.reshape(1, rows, HQ * HD)


def solution(mesh):
    return jax.shard_map(
        per_device,
        mesh=mesh,
        in_specs=(
            P("replica", None),
            P("section", None),
            P("section", "replica", None, None, None),
            P("section", "replica", None, None, None, None),
            P("replica"),
            P("replica", None),
        ),
        out_specs=P("section", "replica", None),
        check_vma=False,
    )
```

```python
import functools
import math

import jax
import jax.numpy as jnp
from jax import lax
from jax.experimental import pallas as pl
from jax.experimental.pallas import tpu as pltpu
from jax.sharding import PartitionSpec as P

HQ = 64
KVH = 4
HD = 128
BLK = 128
NB = 2
GROUP = HQ // KVH
HALF = 8
MID = 4
PLANES = 4
MESH = pl.DeviceIdType.MESH


def dot_t(a, b):
    return lax.dot_general(a, b, (((1,), (1,)), ((), ())), preferred_element_type=jnp.float32)


def dot(a, b):
    return jnp.dot(a, b, preferred_element_type=jnp.float32)


def layer_row(x, gain, kv, slots, length, new):
    xf = x.astype(jnp.float32)
    q = (xf * gain).astype(jnp.bfloat16)
    square = jnp.sum(jnp.sum(xf * xf, axis=0, keepdims=True), axis=1, keepdims=True)
    factor = lax.rsqrt(square * (1.0 / (HQ * HD)) + 1e-05) * (math.log2(math.e) / HD**0.5)
    heads = [slice(h * GROUP, (h + 1) * GROUP) for h in range(KVH)]
    pad = jnp.zeros((BLK - 2 * KVH, HD), jnp.float32)
    new_keys, new_values = [
        jnp.concatenate([new[i], pad], axis=0).astype(jnp.bfloat16) for i in range(2)
    ]
    pos = lax.broadcasted_iota(jnp.int32, (1, BLK), 1)
    own = lax.broadcasted_iota(jnp.int32, (HQ, BLK), 0) // GROUP
    masks = [pos + j * BLK < length for j in range(NB)]
    masks.append(lax.broadcasted_iota(jnp.int32, (HQ, BLK), 1) == own)
    cached = jnp.concatenate(
        [
            dot(q[rows], jnp.concatenate([kv[slots[j], 0, h] for j in range(NB)], axis=1))
            for h, rows in enumerate(heads)
        ],
        axis=0,
    )
    scores = [cached[:, j * BLK : (j + 1) * BLK] for j in range(NB)]
    scores.append(dot_t(q, new_keys))
    scores = [part + jnp.where(mask, 0.0, -1e30) for part, mask in zip(scores, masks)]
    top = jnp.max(functools.reduce(jnp.maximum, scores), axis=1, keepdims=True)
    expos = [jnp.exp2((part - top) * factor) for part in scores]
    total = jnp.sum(sum(expos), axis=1, keepdims=True)
    weights = [part.astype(jnp.bfloat16) for part in expos]
    cached = jnp.concatenate(weights[:NB], axis=1)
    attended = dot(weights[NB], new_values) + jnp.concatenate(
        [
            dot(cached[rows], jnp.concatenate([kv[slots[j], 1, h] for j in range(NB)], axis=0))
            for h, rows in enumerate(heads)
        ],
        axis=0,
    )
    return (xf + attended / total).astype(jnp.bfloat16)


def kernel(
    sections, replicas, rows,
    meta_ref, hidden_ref, new_ref, gain_ref, parked_ref, out_ref,
    park, send, stage, kv_even, kv_odd, metav, metas, hidden, hidden_f, first, x_in, x_out,
    new_raw, new_own, new_in, gains,
    local_sem, meta_send, meta_recv, side_send, stage_recv, pass_send, own_send, kv_recv,
    x_send, x_recv, out_send, out_recv, first_send, new_send, new_recv, gain_send, gain_recv,
):
    s = lax.axis_index("section")
    p = lax.axis_index("replica")
    core = lax.rem(p, 2)
    chip = p // 2
    width = sections // PLANES
    plane = s // width
    worker = core == 1
    side = width * (1 - 2 * lax.rem(chip, 2))

    def at(shift):
        return lax.rem(p + shift + 2 * replicas, replicas)

    def sec(shift):
        return lax.rem(s + shift + 2 * sections, sections)

    def remote(src, dst, send_sem, recv_sem, section, replica):
        return pltpu.make_async_remote_copy(
            src, dst, send_sem, recv_sem,
            device_id={"section": section, "replica": replica}, device_id_type=MESH,
        )

    def local(i, src, dst):
        return pltpu.make_async_copy(src, dst, local_sem.at[i])

    fetch = [
        local(0, parked_ref, park),
        local(1, hidden_ref, hidden),
        local(2, new_ref, new_raw),
        local(3, gain_ref, gains.at[1]),
    ]
    for copy in fetch:
        copy.start()

    barrier = pltpu.get_barrier_semaphore()

    def greet(section, replica):
        pl.semaphore_signal(
            barrier, inc=1, device_id={"section": section, "replica": replica}, device_id_type=MESH
        )

    @pl.loop(1, replicas)
    def _(j):
        greet(s, at(j))

    greet(sec(width), p)
    greet(sec(-width), p)

    @pl.when(worker)
    def _():
        greet(sec(-side), at(-1))
        greet(sec(-side), at(MID - 1))
        greet(sec(-1), p)

    @pl.when(core == 0)
    def _():
        greet(sec(side), at(HALF + MID + 1))

    pl.semaphore_wait(barrier, replicas - 1 + 2 + 2)

    def meta_copy(k):
        return remote(
            meta_ref, metav.at[k], meta_send.at[k], meta_recv.at[k], s, at(HALF + k)
        )

    my_section = sec(side * (1 - core))
    mine = at(HALF + MID + 1 - core)

    def first_copy(m):
        return remote(
            first.at[m], x_in.at[core * rows + m], first_send.at[m], x_recv.at[core * rows + m],
            my_section, mine,
        )

    new_copy = remote(
        new_own, new_in.at[core], new_send, new_recv.at[core], my_section, mine
    )
    gain_copy = remote(gain_ref, gains.at[0], gain_send, gain_recv, sec(side), p)

    @pl.loop(0, HALF)
    def _(k):
        meta_copy(k).start()

    @pl.loop(0, HALF)
    def _(k):
        meta_copy(k).wait_recv()

    to_smem = local(4, metav, metas)
    to_smem.start()
    to_smem.wait()
    fetch[0].wait()

    def even(e):
        return 2 * e + core

    def odd(e):
        return 2 * e + 1 - core

    def target(k):
        to = p + MID - k + 2 * replicas
        return lax.rem(to - lax.rem(to, 2) + 1, replicas)

    def unit(k):
        return send.at[pl.ds(NB * k, NB)]

    def held(home, k):
        return (kv_even, kv_odd)[home].at[pl.ds(NB * k, NB)]

    def pick(k):
        for j in range(NB):
            block = metas[k, 0, NB * k + j]
            for h in range(KVH):
                send[NB * k + j, 0, h] = park[block, 0, h].T
                send[NB * k + j, 1, h] = park[block, 1, h]

    def side_copy(e):
        to = sec(side * (1 - 2 * lax.rem(e, 2)))
        return remote(unit(even(e)), stage.at[e], side_send.at[e], stage_recv.at[e], to, p)

    def near_copy(e=2):
        k = even(e)
        return remote(
            unit(k), held(0, k), side_send.at[e], kv_recv.at[0, k], sec(side), target(k)
        )

    def pass_copy(e):
        k = even(e)
        return remote(stage.at[e], held(0, k), pass_send.at[e], kv_recv.at[0, k], s, target(k))

    def own_copy(e):
        k = odd(e)
        return remote(unit(k), held(1, k), own_send.at[e], kv_recv.at[1, k], s, target(k))

    def own_stay(e):
        k = odd(e)
        return pltpu.make_async_copy(unit(k), held(1, k), kv_recv.at[1, k])

    def own_start_one(e):
        @pl.when(target(odd(e)) != p)
        def _():
            own_copy(e).start()

        @pl.when(target(odd(e)) == p)
        def _():
            own_stay(e).start()

    def own_start():
        @pl.loop(0, 4)
        def _(e):
            own_start_one(e)

    def own_wait():
        @pl.loop(0, 4)
        def _(e):
            @pl.when(target(odd(e)) != p)
            def _():
                own_copy(e).wait_send()

    def pass_start_one(e):
        side_copy(e).wait_recv()
        pass_copy(e).start()

    def from_plane(step, zero, one):
        @pl.when(side == -step * width)
        def _():
            zero(0)

        @pl.when(side == step * width)
        def _():
            one(1)
            one(3)

    def pass_start(step):
        from_plane(step, pass_start_one, pass_start_one)

    def pass_wait(step):
        def wait(e):
            pass_copy(e).wait_send()

        from_plane(step, wait, wait)

    @pl.loop(0, 2)
    def _(e):
        pick(even(e))
        side_copy(e).start()

    @pl.loop(0, 4)
    def _(e):
        pick(odd(e))

        @pl.when(plane == 0)
        def _():
            own_start_one(e)

    pick(even(3))
    pick(even(2))

    fetch[1].wait()
    fetch[2].wait()
    fetch[3].wait()

    @pl.loop(0, rows)
    def _(m):
        pair = new_raw[0, m].astype(jnp.float32)
        new_own[m, 0] = jnp.concatenate([pair[0], pair[1]], axis=0)
        new_own[m, 1] = jnp.concatenate([pair[1], pair[0]], axis=0)

    new_copy.start()

    @pl.when(worker)
    def _():
        gain_copy.start()

    @pl.when(s == 0)
    def _():
        for h in range(HQ):
            hidden_f[:, h, :] = hidden[:, h * HD : (h + 1) * HD].astype(jnp.float32)

        @pl.loop(0, rows)
        def _(m):
            first[m] = hidden_f[m].astype(jnp.bfloat16)
            first_copy(m).start()

    side_copy(0).wait_send()
    near_copy().start()
    side_copy(1).wait_send()
    side_copy(3).start()

    last_plane = PLANES - 1

    @pl.when(plane == 0)
    def _():
        own_wait()
        pass_start(1)

    @pl.when((plane > 0) & (plane < last_plane))
    def _():
        pass_start(-1)
        pass_wait(-1)
        own_start()

    @pl.when(plane == last_plane)
    def _():
        pass_start(1)
        pass_wait(1)
        pass_start(-1)

    def third():
        @pl.when(plane == 0)
        def _():
            pass_wait(1)
            pass_start(-1)
            pass_wait(-1)

        @pl.when((plane > 0) & (plane < last_plane))
        def _():
            own_wait()
            pass_start(1)
            pass_wait(1)

        @pl.when(plane == last_plane)
        def _():
            pass_wait(-1)
            own_start()
            own_wait()

    def relay_copy(i, section):
        return remote(x_out.at[i], x_in.at[i], x_send.at[i], x_recv.at[i], section, p)

    def home_copy(home, m, section, replica):
        return remote(
            x_out.at[home * rows + m], out_ref.at[m], out_send.at[home * rows + m], out_recv.at[m],
            section, replica,
        )

    def work(home):
        layer = sec(-side * (1 - home))
        remote(new_own, new_in.at[home], new_send, new_recv.at[home], s, p).wait_recv()

        if home == 0:
            gain_copy.wait_recv()

        @pl.loop(0, HALF)
        def _(k):
            remote(unit(k), held(home, k), own_send.at[0], kv_recv.at[home, k], s, p).wait_recv()

        @pl.loop(0, rows)
        def _(m):
            i = home * rows + m
            info = MID + 1 - home
            relay_copy(i, s).wait_recv()
            slots = [metas[info, 1, j * rows + m] for j in range(NB)]
            length = metas[info, 2, m]
            x_out[i] = layer_row(
                x_in[i], gains[home], (kv_even, kv_odd)[home], slots, length, new_in[home, m]
            )

            @pl.when(layer < sections - 1)
            def _():
                relay_copy(i, sec(1)).start()

            home_copy(home, m, layer, at(MID - 1 + home)).start()

    def work_wait(home):
        layer = sec(-side * (1 - home))

        @pl.loop(0, rows)
        def _(m):
            @pl.when(layer < sections - 1)
            def _():
                relay_copy(home * rows + m, sec(1)).wait_send()

            home_copy(home, m, layer, at(MID - 1 + home)).wait_send()

    other = sec(-side)
    early = jnp.minimum(s, other) < width
    odd_first = (other > s).astype(jnp.int32)
    third_turn = jnp.where(worker & early, 2 - odd_first, 0)

    @pl.loop(0, 3)
    def _(turn):
        @pl.when(turn == third_turn)
        def _():
            third()

        @pl.when(worker & (turn == 1))
        def _():
            work(0)

        @pl.when(worker & (turn == 2 - 2 * odd_first))
        def _():
            work(1)

    @pl.when(worker)
    def _():
        work_wait(0)
        work_wait(1)
        gain_copy.wait_send()

    @pl.loop(0, HALF)
    def _(k):
        meta_copy(k).wait_send()

    near_copy().wait_send()
    side_copy(3).wait_send()
    new_copy.wait_send()

    @pl.loop(0, rows)
    def _(m):
        @pl.when(s == 0)
        def _():
            first_copy(m).wait_send()

        home_copy(0, m, s, p).wait_recv()


def per_device(hidden_in, norm_gain, new_kv, parked, cache_len, block_home):
    replicas = lax.axis_size("replica")
    sections = lax.axis_size("section")
    me = lax.axis_index("replica")
    blocks = parked[0]
    park_count = blocks.shape[0]
    rows = block_home.shape[0]
    count = rows * NB

    flat = block_home.T.reshape(count)
    near = lax.rem(flat - (me + HALF) * park_count + 2 * replicas * park_count, replicas * park_count)
    place = jnp.sum((near[None, :] < near[:, None]).astype(jnp.int32), axis=1)
    hit = place[None, :] == jnp.arange(count, dtype=jnp.int32)[:, None]
    local = jnp.sum(jnp.where(hit, lax.rem(flat, park_count)[None, :], 0), axis=1)
    meta = jnp.stack([
        jnp.pad(local, (0, 128 - count)),
        jnp.pad(place, (0, 128 - count)),
        jnp.pad(cache_len, (0, 128 - rows)),
    ])
    meta = jnp.pad(meta, ((0, 5), (0, 0)))

    total = 2 * rows
    hbm = pl.BlockSpec(memory_space=pl.ANY)
    dma = pltpu.SemaphoreType.DMA
    out = pl.pallas_call(
        functools.partial(kernel, sections, replicas, rows),
        out_shape=jax.ShapeDtypeStruct((rows, HQ, HD), jnp.bfloat16),
        in_specs=[hbm] * 5,
        out_specs=hbm,
        scratch_shapes=[
            pltpu.VMEM(blocks.shape, jnp.bfloat16),
            pltpu.VMEM(blocks.shape, jnp.bfloat16),
            pltpu.VMEM((4, NB) + blocks.shape[1:], jnp.bfloat16),
            pltpu.VMEM(blocks.shape, jnp.bfloat16),
            pltpu.VMEM(blocks.shape, jnp.bfloat16),
            pltpu.VMEM((HALF, 8, 128), jnp.int32),
            pltpu.SMEM((HALF, 8, 128), jnp.int32),
            pltpu.VMEM(hidden_in.shape, jnp.bfloat16),
            pltpu.VMEM((rows, HQ, HD), jnp.float32),
            pltpu.VMEM((rows, HQ, HD), jnp.bfloat16),
            pltpu.VMEM((total, HQ, HD), jnp.bfloat16),
            pltpu.VMEM((total, HQ, HD), jnp.bfloat16),
            pltpu.VMEM(new_kv.shape, jnp.bfloat16),
            pltpu.VMEM((rows, 2, 2 * KVH, HD), jnp.float32),
            pltpu.VMEM((2, rows, 2, 2 * KVH, HD), jnp.float32),
            pltpu.VMEM((2, HQ, HD), jnp.float32),
            dma((5,)),
            dma((HALF,)), dma((HALF,)), dma((4,)), dma((4,)), dma((4,)), dma((4,)), dma((2, HALF)),
            dma((total,)), dma((total,)), dma((total,)), dma((rows,)),
            dma((rows,)), dma, dma((2,)), dma, dma,
        ],
        compiler_params=pltpu.CompilerParams(
            collective_id=0, has_side_effects=True, vmem_limit_bytes=56 * 1024 * 1024
        ),
    )(meta, hidden_in, new_kv, norm_gain.reshape(HQ, HD), blocks)
    return out.reshape(1, rows, HQ * HD)


def solution(mesh):
    return jax.shard_map(
        per_device,
        mesh=mesh,
        in_specs=(
            P("replica", None),
            P("section", None),
            P("section", "replica", None, None, None),
            P("section", "replica", None, None, None, None),
            P("replica"),
            P("replica", None),
        ),
        out_specs=P("section", "replica", None),
        check_vma=False,
    )
```

```python
import functools
import math

import jax
import jax.numpy as jnp
from jax import lax
from jax.experimental import pallas as pl
from jax.experimental.pallas import tpu as pltpu
from jax.sharding import PartitionSpec as P

HQ = 64
KVH = 4
HD = 128
BLK = 128
NB = 2
GROUP = HQ // KVH
HALF = 8
MID = 4
PLANES = 4
MESH = pl.DeviceIdType.MESH


def dot_t(a, b):
    return lax.dot_general(a, b, (((1,), (1,)), ((), ())), preferred_element_type=jnp.float32)


def dot(a, b):
    return jnp.dot(a, b, preferred_element_type=jnp.float32)


def layer_row(x, gain, kv, slots, length, new):
    xf = x.astype(jnp.float32)
    q = (xf * gain).astype(jnp.bfloat16)
    square = jnp.sum(jnp.sum(xf * xf, axis=0, keepdims=True), axis=1, keepdims=True)
    factor = lax.rsqrt(square * (1.0 / (HQ * HD)) + 1e-05) * (math.log2(math.e) / HD**0.5)
    heads = [slice(h * GROUP, (h + 1) * GROUP) for h in range(KVH)]
    pad = jnp.zeros((BLK - 2 * KVH, HD), jnp.float32)
    new_keys, new_values = [
        jnp.concatenate([new[i], pad], axis=0).astype(jnp.bfloat16) for i in range(2)
    ]
    pos = lax.broadcasted_iota(jnp.int32, (1, BLK), 1)
    own = lax.broadcasted_iota(jnp.int32, (HQ, BLK), 0) // GROUP
    masks = [pos + j * BLK < length for j in range(NB)]
    masks.append(lax.broadcasted_iota(jnp.int32, (HQ, BLK), 1) == own)
    cached = jnp.concatenate(
        [
            dot(q[rows], jnp.concatenate([kv[slots[j], 0, h] for j in range(NB)], axis=1))
            for h, rows in enumerate(heads)
        ],
        axis=0,
    )
    scores = [cached[:, j * BLK : (j + 1) * BLK] for j in range(NB)]
    scores.append(dot_t(q, new_keys))
    scores = [part + jnp.where(mask, 0.0, -1e30) for part, mask in zip(scores, masks)]
    top = jnp.max(functools.reduce(jnp.maximum, scores), axis=1, keepdims=True)
    expos = [jnp.exp2((part - top) * factor) for part in scores]
    total = jnp.sum(sum(expos), axis=1, keepdims=True)
    weights = [part.astype(jnp.bfloat16) for part in expos]
    cached = jnp.concatenate(weights[:NB], axis=1)
    attended = dot(weights[NB], new_values) + jnp.concatenate(
        [
            dot(cached[rows], jnp.concatenate([kv[slots[j], 1, h] for j in range(NB)], axis=0))
            for h, rows in enumerate(heads)
        ],
        axis=0,
    )
    return (xf + attended / total).astype(jnp.bfloat16)


def kernel(
    sections, replicas, rows,
    table_ref, length_ref, hidden_ref, new_ref, gain_ref, parked_ref, out_ref,
    park, send, stage, kv_even, kv_odd, table, lengths, meta, metav, metas, hidden, hidden_f, first, x_in, x_out,
    new_raw, new_own, new_in, gains,
    local_sem, meta_send, meta_recv, side_send, stage_recv, pass_send, own_send, even_recv, odd_recv,
    x_send, x_recv, out_send, out_recv, first_send, new_send, new_recv, gain_send, gain_recv,
):
    s = lax.axis_index("section")
    p = lax.axis_index("replica")
    core = lax.rem(p, 2)
    chip = p // 2
    width = sections // PLANES
    plane = s // width
    worker = core == 1
    side = width * (1 - 2 * lax.rem(chip, 2))

    def at(shift):
        return lax.rem(p + shift + 2 * replicas, replicas)

    def sec(shift):
        return lax.rem(s + shift + 2 * sections, sections)

    def remote(src, dst, send_sem, recv_sem, section, replica):
        return pltpu.make_async_remote_copy(
            src, dst, send_sem, recv_sem,
            device_id={"section": section, "replica": replica}, device_id_type=MESH,
        )

    def local(i, src, dst):
        return pltpu.make_async_copy(src, dst, local_sem.at[i])

    fetch = [
        local(0, parked_ref, park),
        local(1, hidden_ref, hidden),
        local(2, new_ref, new_raw),
        local(3, gain_ref, gains.at[1]),
        local(4, table_ref, table),
        local(5, length_ref, lengths),
    ]
    for copy in fetch:
        copy.start()

    barrier = pltpu.get_barrier_semaphore()

    def greet(section, replica):
        pl.semaphore_signal(
            barrier, inc=1, device_id={"section": section, "replica": replica}, device_id_type=MESH
        )

    @pl.loop(1, replicas)
    def _(j):
        greet(s, at(j))

    greet(sec(width), p)
    greet(sec(-width), p)

    @pl.when(worker)
    def _():
        greet(sec(-side), at(-1))
        greet(sec(-side), at(MID - 1))
        greet(sec(-1), p)

    @pl.when(core == 0)
    def _():
        greet(sec(side), at(HALF + MID + 1))

    count = NB * rows
    parks = park.shape[0]
    fetch[4].wait()
    fetch[5].wait()
    blocks = [table[j, m] for j in range(NB) for m in range(rows)]
    near = [
        lax.rem(b - (p + HALF) * parks + 2 * replicas * parks, replicas * parks) for b in blocks
    ]
    row = lax.broadcasted_iota(jnp.int32, meta.shape, 0)
    lane = lax.broadcasted_iota(jnp.int32, meta.shape, 1)
    info = jnp.zeros(meta.shape, jnp.int32)
    for e in range(count):
        place = sum((near[i] < near[e]).astype(jnp.int32) for i in range(count) if i != e)
        info = jnp.where((row == 0) & (lane == place), lax.rem(blocks[e], parks), info)
        info = jnp.where((row == 1) & (lane == e), place, info)
    for m in range(rows):
        info = jnp.where((row == 2) & (lane == m), lengths[0, m], info)
    meta[...] = info

    def turn_keys(b):
        for h in range(KVH):
            park[b, 0, h] = park[b, 0, h].T

    fetch[0].wait()
    pl.loop(0, parks // 2)(turn_keys)

    pl.semaphore_wait(barrier, replicas - 1 + 2 + 2)

    def meta_copy(k):
        return remote(
            meta, metav.at[k], meta_send.at[k], meta_recv.at[k], s, at(HALF + k)
        )

    my_section = sec(side * (1 - core))
    mine = at(HALF + MID + 1 - core)

    def first_copy(m):
        return remote(
            first.at[m], x_in.at[core * rows + m], first_send.at[m], x_recv.at[core * rows + m],
            my_section, mine,
        )

    new_copy = remote(
        new_own, new_in.at[core], new_send, new_recv.at[core], my_section, mine
    )
    gain_copy = remote(gain_ref, gains.at[0], gain_send, gain_recv, sec(side), p)

    @pl.loop(0, HALF)
    def _(k):
        meta_copy(k).start()

    pl.loop(parks // 2, parks)(turn_keys)

    def meta_wait(first, last):
        @pl.loop(first, last)
        def _(k):
            meta_copy(k).wait_recv()

        some = pl.ds(first, last - first)
        to_smem = local(6, metav.at[some], metas.at[some])
        to_smem.start()
        to_smem.wait()

    def even(e):
        return 2 * e + core

    def odd(e):
        return 2 * e + 1 - core

    def target(k):
        to = p + MID - k + 2 * replicas
        return lax.rem(to - lax.rem(to, 2) + 1, replicas)

    def unit(k):
        return send.at[pl.ds(NB * k, NB)]

    def held(home, k):
        return (kv_even, kv_odd)[home].at[pl.ds(NB * k, NB)]

    def pick(k):
        for j in range(NB):
            block = metas[k, 0, NB * k + j]
            for h in range(KVH):
                send[NB * k + j, 0, h] = park[block, 0, h]
                send[NB * k + j, 1, h] = park[block, 1, h]

    def piece(k, j):
        return send.at[pl.ds(NB * k + j, 1)], kv_even.at[pl.ds(NB * k + j, 1)], even_recv.at[k, j]

    def side_copy(e, j):
        to = sec(side * (1 - 2 * lax.rem(e, 2)))
        src, _, _ = piece(even(e), j)
        return remote(
            src, stage.at[e, pl.ds(j, 1)], side_send.at[e, j], stage_recv.at[e, j], to, p
        )

    def near_copy(j, e=2):
        src, dst, sem = piece(even(e), j)
        return remote(src, dst, side_send.at[e, j], sem, sec(side), target(even(e)))

    def pass_copy(e, j):
        _, dst, sem = piece(even(e), j)
        return remote(
            stage.at[e, pl.ds(j, 1)], dst, pass_send.at[e, j], sem, s, target(even(e))
        )

    def own_copy(e):
        k = odd(e)
        return remote(unit(k), held(1, k), own_send.at[e], odd_recv.at[k], s, target(k))

    def own_stay(e):
        k = odd(e)
        return pltpu.make_async_copy(unit(k), held(1, k), odd_recv.at[k])

    def own_start_one(e):
        @pl.when(target(odd(e)) != p)
        def _():
            own_copy(e).start()

        @pl.when(target(odd(e)) == p)
        def _():
            own_stay(e).start()

    def own_wait():
        @pl.loop(0, 4)
        def _(e):
            @pl.when(target(odd(e)) != p)
            def _():
                own_copy(e).wait_send()

    def pass_start_one(e):
        for j in range(NB):
            side_copy(e, j).wait_recv()
            pass_copy(e, j).start()

    def from_plane(step, zero, one):
        @pl.when(side == -step * width)
        def _():
            zero(0)

        @pl.when(side == step * width)
        def _():
            one(3)
            one(1)

    def pass_start(step):
        from_plane(step, pass_start_one, pass_start_one)

    def pass_wait(step):
        def wait(e):
            for j in range(NB):
                pass_copy(e, j).wait_send()

        from_plane(step, wait, wait)

    waits = lax.rem(plane, 2) == 1

    def goes_first(e):
        return jnp.logical_not(waits) | (e == 3 * (1 - core))

    meta_wait(HALF - 2, HALF)
    pick(even(3))
    for j in range(NB):
        side_copy(3, j).start()

    meta_wait(0, HALF - 2)
    pick(even(0))
    for j in range(NB):
        side_copy(0, j).start()

    @pl.loop(0, 4)
    def _(e):
        pick(odd(e))

        @pl.when(goes_first(e))
        def _():
            own_start_one(e)

    pick(even(1))
    pick(even(2))

    fetch[1].wait()
    fetch[2].wait()
    fetch[3].wait()

    @pl.loop(0, rows)
    def _(m):
        pair = new_raw[0, m].astype(jnp.float32)
        new_own[m, 0] = jnp.concatenate([pair[0], pair[1]], axis=0)
        new_own[m, 1] = jnp.concatenate([pair[1], pair[0]], axis=0)

    new_copy.start()

    @pl.when(worker)
    def _():
        gain_copy.start()

    @pl.when(s == 0)
    def _():
        for h in range(HQ):
            hidden_f[:, h, :] = hidden[:, h * HD : (h + 1) * HD].astype(jnp.float32)

        @pl.loop(0, rows)
        def _(m):
            first[m] = hidden_f[m].astype(jnp.bfloat16)
            first_copy(m).start()

    for j in range(NB):
        side_copy(3, j).wait_send()
        side_copy(1, j).start()
        side_copy(0, j).wait_send()
        near_copy(j).start()

    lead = jnp.where((plane == 0) | (plane == PLANES - 1), 1, -1)

    @pl.when(plane == 0)
    def _():
        own_wait()

    pass_start(lead)

    @pl.when(waits)
    def _():
        pass_wait(lead)

        @pl.loop(0, 4)
        def _(e):
            @pl.when(jnp.logical_not(goes_first(e)))
            def _():
                own_start_one(e)

    def passes_left():
        @pl.when(jnp.logical_not(waits))
        def _():
            pass_wait(lead)

        pass_start(-lead)

    def relay_copy(i, section):
        return remote(x_out.at[i], x_in.at[i], x_send.at[i], x_recv.at[i], section, p)

    def home_copy(home, m, section, replica):
        return remote(
            x_out.at[home * rows + m], out_ref.at[m], out_send.at[home * rows + m], out_recv.at[m],
            section, replica,
        )

    def work(home):
        layer = sec(-side * (1 - home))
        remote(new_own, new_in.at[home], new_send, new_recv.at[home], s, p).wait_recv()

        if home == 0:
            gain_copy.wait_recv()

        @pl.loop(0, HALF)
        def _(k):
            if home == 0:
                for j in range(NB):
                    src, dst, sem = piece(k, j)
                    remote(src, dst, side_send.at[0, j], sem, s, p).wait_recv()
            else:
                remote(unit(k), held(1, k), own_send.at[0], odd_recv.at[k], s, p).wait_recv()

        @pl.loop(0, rows)
        def _(m):
            i = home * rows + m
            info = MID + 1 - home
            relay_copy(i, s).wait_recv()
            slots = [metas[info, 1, j * rows + m] for j in range(NB)]
            length = metas[info, 2, m]
            x_out[i] = layer_row(
                x_in[i], gains[home], (kv_even, kv_odd)[home], slots, length, new_in[home, m]
            )

            @pl.when(layer < sections - 1)
            def _():
                relay_copy(i, sec(1)).start()

            home_copy(home, m, layer, at(MID - 1 + home)).start()

    def work_wait(home):
        layer = sec(-side * (1 - home))

        @pl.loop(0, rows)
        def _(m):
            @pl.when(layer < sections - 1)
            def _():
                relay_copy(home * rows + m, sec(1)).wait_send()

            home_copy(home, m, layer, at(MID - 1 + home)).wait_send()

    other = sec(-side)
    early = jnp.minimum(s, other) < width
    odd_first = (other > s).astype(jnp.int32)
    left_turn = jnp.where(worker & early, 2 - odd_first, 0)

    @pl.loop(0, 3)
    def _(turn):
        @pl.when(turn == left_turn)
        def _():
            passes_left()

        @pl.when(worker & (turn == 1))
        def _():
            work(0)

        @pl.when(worker & (turn == 2 - 2 * odd_first))
        def _():
            work(1)

    @pl.when(worker)
    def _():
        work_wait(0)
        work_wait(1)
        gain_copy.wait_send()

    @pl.loop(0, HALF)
    def _(k):
        meta_copy(k).wait_send()

    for j in range(NB):
        near_copy(j).wait_send()
        side_copy(1, j).wait_send()

    pass_wait(-lead)

    @pl.when(plane > 0)
    def _():
        own_wait()

    new_copy.wait_send()

    @pl.loop(0, rows)
    def _(m):
        @pl.when(s == 0)
        def _():
            first_copy(m).wait_send()

        home_copy(0, m, s, p).wait_recv()


def per_device(hidden_in, norm_gain, new_kv, parked, cache_len, block_home):
    replicas = lax.axis_size("replica")
    sections = lax.axis_size("section")
    blocks = parked[0]
    rows = block_home.shape[0]
    total = 2 * rows
    hbm = pl.BlockSpec(memory_space=pl.ANY)
    dma = pltpu.SemaphoreType.DMA
    out = pl.pallas_call(
        functools.partial(kernel, sections, replicas, rows),
        out_shape=jax.ShapeDtypeStruct((rows, HQ, HD), jnp.bfloat16),
        in_specs=[hbm] * 6,
        out_specs=hbm,
        scratch_shapes=[
            pltpu.VMEM(blocks.shape, jnp.bfloat16),
            pltpu.VMEM(blocks.shape, jnp.bfloat16),
            pltpu.VMEM((4, NB) + blocks.shape[1:], jnp.bfloat16),
            pltpu.VMEM(blocks.shape, jnp.bfloat16),
            pltpu.VMEM(blocks.shape, jnp.bfloat16),
            pltpu.SMEM((NB, rows), jnp.int32),
            pltpu.SMEM((1, rows), jnp.int32),
            pltpu.VMEM((8, 128), jnp.int32),
            pltpu.VMEM((HALF, 8, 128), jnp.int32),
            pltpu.SMEM((HALF, 8, 128), jnp.int32),
            pltpu.VMEM(hidden_in.shape, jnp.bfloat16),
            pltpu.VMEM((rows, HQ, HD), jnp.float32),
            pltpu.VMEM((rows, HQ, HD), jnp.bfloat16),
            pltpu.VMEM((total, HQ, HD), jnp.bfloat16),
            pltpu.VMEM((total, HQ, HD), jnp.bfloat16),
            pltpu.VMEM(new_kv.shape, jnp.bfloat16),
            pltpu.VMEM((rows, 2, 2 * KVH, HD), jnp.float32),
            pltpu.VMEM((2, rows, 2, 2 * KVH, HD), jnp.float32),
            pltpu.VMEM((2, HQ, HD), jnp.float32),
            dma((7,)),
            dma((HALF,)), dma((HALF,)), dma((4, NB)), dma((4, NB)), dma((4, NB)), dma((4,)),
            dma((HALF, NB)), dma((HALF,)),
            dma((total,)), dma((total,)), dma((total,)), dma((rows,)),
            dma((rows,)), dma, dma((2,)), dma, dma,
        ],
        compiler_params=pltpu.CompilerParams(
            collective_id=0, has_side_effects=True, vmem_limit_bytes=56 * 1024 * 1024
        ),
    )(block_home.T, cache_len.reshape(1, rows), hidden_in, new_kv, norm_gain.reshape(HQ, HD), blocks)
    return out.reshape(1, rows, HQ * HD)


def solution(mesh):
    return jax.shard_map(
        per_device,
        mesh=mesh,
        in_specs=(
            P("replica", None),
            P("section", None),
            P("section", "replica", None, None, None),
            P("section", "replica", None, None, None, None),
            P("replica"),
            P("replica", None),
        ),
        out_specs=P("section", "replica", None),
        check_vma=False,
    )
```

```python
import functools
import math

import jax
import jax.numpy as jnp
from jax import lax
from jax.experimental import pallas as pl
from jax.experimental.pallas import tpu as pltpu
from jax.sharding import PartitionSpec as P

HQ = 64
KVH = 4
HD = 128
BLK = 128
NB = 2
GROUP = HQ // KVH
HALF = 8
MID = 4
PLANES = 4
MESH = pl.DeviceIdType.MESH


def dot_t(a, b):
    return lax.dot_general(a, b, (((1,), (1,)), ((), ())), preferred_element_type=jnp.float32)


def dot(a, b):
    return jnp.dot(a, b, preferred_element_type=jnp.float32)


def layer_row(x, gain, kv, slots, length, new):
    xf = x.astype(jnp.float32)
    q = (xf * gain).astype(jnp.bfloat16)
    square = jnp.sum(jnp.sum(xf * xf, axis=0, keepdims=True), axis=1, keepdims=True)
    factor = lax.rsqrt(square * (1.0 / (HQ * HD)) + 1e-05) * (math.log2(math.e) / HD**0.5)
    heads = [slice(h * GROUP, (h + 1) * GROUP) for h in range(KVH)]
    pad = jnp.zeros((BLK - 2 * KVH, HD), jnp.float32)
    new_keys, new_values = [
        jnp.concatenate([new[i], pad], axis=0).astype(jnp.bfloat16) for i in range(2)
    ]
    pos = lax.broadcasted_iota(jnp.int32, (1, BLK), 1)
    own = lax.broadcasted_iota(jnp.int32, (HQ, BLK), 0) // GROUP
    masks = [pos + j * BLK < length for j in range(NB)]
    masks.append(lax.broadcasted_iota(jnp.int32, (HQ, BLK), 1) == own)
    cached = jnp.concatenate(
        [
            dot(q[rows], jnp.concatenate([kv[slots[j], 0, h] for j in range(NB)], axis=1))
            for h, rows in enumerate(heads)
        ],
        axis=0,
    )
    scores = [cached[:, j * BLK : (j + 1) * BLK] for j in range(NB)]
    scores.append(dot_t(q, new_keys))
    scores = [part + jnp.where(mask, 0.0, -1e30) for part, mask in zip(scores, masks)]
    top = jnp.max(functools.reduce(jnp.maximum, scores), axis=1, keepdims=True)
    expos = [jnp.exp2((part - top) * factor) for part in scores]
    total = jnp.sum(sum(expos), axis=1, keepdims=True)
    weights = [part.astype(jnp.bfloat16) for part in expos]
    cached = jnp.concatenate(weights[:NB], axis=1)
    attended = dot(weights[NB], new_values) + jnp.concatenate(
        [
            dot(cached[rows], jnp.concatenate([kv[slots[j], 1, h] for j in range(NB)], axis=0))
            for h, rows in enumerate(heads)
        ],
        axis=0,
    )
    return (xf + attended / total).astype(jnp.bfloat16)


def kernel(
    sections, replicas, rows,
    table_ref, length_ref, hidden_ref, new_ref, gain_ref, parked_ref, out_ref,
    park, send, stage, kv_even, kv_odd, table, lengths, meta, metav, metas, hidden, hidden_f, first, x_in, x_out,
    new_raw, new_own, new_in, gains,
    local_sem, meta_send, meta_recv, side_send, stage_recv, pass_send, own_send, even_recv, odd_recv,
    x_send, x_recv, out_send, out_recv, first_send, new_send, new_recv, gain_send, gain_recv,
):
    s = lax.axis_index("section")
    p = lax.axis_index("replica")
    core = lax.rem(p, 2)
    chip = p // 2
    width = sections // PLANES
    plane = s // width
    worker = core == 1
    side = width * (2 * lax.rem(chip, 2) - 1)

    def at(shift):
        return lax.rem(p + shift + 2 * replicas, replicas)

    def sec(shift):
        return lax.rem(s + shift + 2 * sections, sections)

    def remote(src, dst, send_sem, recv_sem, section, replica):
        return pltpu.make_async_remote_copy(
            src, dst, send_sem, recv_sem,
            device_id={"section": section, "replica": replica}, device_id_type=MESH,
        )

    def local(i, src, dst):
        return pltpu.make_async_copy(src, dst, local_sem.at[i])

    fetch = [
        local(0, parked_ref, park),
        local(1, hidden_ref, hidden),
        local(2, new_ref, new_raw),
        local(3, gain_ref, gains.at[1]),
        local(4, table_ref, table),
        local(5, length_ref, lengths),
    ]
    for copy in fetch:
        copy.start()

    barrier = pltpu.get_barrier_semaphore()

    def greet(section, replica):
        pl.semaphore_signal(
            barrier, inc=1, device_id={"section": section, "replica": replica}, device_id_type=MESH
        )

    @pl.loop(1, replicas)
    def _(j):
        greet(s, at(j))

    greet(sec(width), p)
    greet(sec(-width), p)

    @pl.when(worker)
    def _():
        greet(sec(-side), at(-1))
        greet(sec(-side), at(MID - 1))
        greet(sec(-1), p)

    @pl.when(core == 0)
    def _():
        greet(sec(side), at(HALF + MID + 1))

    count = NB * rows
    parks = park.shape[0]
    fetch[4].wait()
    fetch[5].wait()
    blocks = [table[j, m] for j in range(NB) for m in range(rows)]
    near = [
        lax.rem(b - (p + HALF) * parks + 2 * replicas * parks, replicas * parks) for b in blocks
    ]
    row = lax.broadcasted_iota(jnp.int32, meta.shape, 0)
    lane = lax.broadcasted_iota(jnp.int32, meta.shape, 1)
    info = jnp.zeros(meta.shape, jnp.int32)
    for e in range(count):
        place = sum((near[i] < near[e]).astype(jnp.int32) for i in range(count) if i != e)
        info = jnp.where((row == 0) & (lane == place), lax.rem(blocks[e], parks), info)
        info = jnp.where((row == 1) & (lane == e), place, info)
    for m in range(rows):
        info = jnp.where((row == 2) & (lane == m), lengths[0, m], info)
    meta[...] = info

    def turn_keys(b):
        for h in range(KVH):
            park[b, 0, h] = park[b, 0, h].T

    fetch[0].wait()
    pl.loop(0, parks // 2)(turn_keys)

    pl.semaphore_wait(barrier, replicas - 1 + 2 + 2)

    def meta_copy(k):
        return remote(
            meta, metav.at[k], meta_send.at[k], meta_recv.at[k], s, at(HALF + k)
        )

    my_section = sec(side * (1 - core))
    mine = at(HALF + MID + 1 - core)

    def first_copy(m):
        return remote(
            first.at[m], x_in.at[core * rows + m], first_send.at[m], x_recv.at[core * rows + m],
            my_section, mine,
        )

    new_copy = remote(
        new_own, new_in.at[core], new_send, new_recv.at[core], my_section, mine
    )
    gain_copy = remote(gain_ref, gains.at[0], gain_send, gain_recv, sec(side), p)

    @pl.loop(0, HALF)
    def _(k):
        meta_copy(k).start()

    pl.loop(parks // 2, parks)(turn_keys)

    def meta_wait(first, last):
        @pl.loop(first, last)
        def _(k):
            meta_copy(k).wait_recv()

        some = pl.ds(first, last - first)
        to_smem = local(6, metav.at[some], metas.at[some])
        to_smem.start()
        to_smem.wait()

    def even(e):
        return 2 * e + core

    def odd(e):
        return 2 * e + 1 - core

    def target(k):
        to = p + MID - k + 2 * replicas
        return lax.rem(to - lax.rem(to, 2) + 1, replicas)

    def unit(k):
        return send.at[pl.ds(NB * k, NB)]

    def held(home, k):
        return (kv_even, kv_odd)[home].at[pl.ds(NB * k, NB)]

    def pick(k):
        for j in range(NB):
            block = metas[k, 0, NB * k + j]
            for h in range(KVH):
                send[NB * k + j, 0, h] = park[block, 0, h]
                send[NB * k + j, 1, h] = park[block, 1, h]

    def piece(k, j):
        return send.at[pl.ds(NB * k + j, 1)], kv_even.at[pl.ds(NB * k + j, 1)], even_recv.at[k, j]

    def side_copy(e, j):
        to = sec(side * (1 - 2 * lax.rem(e, 2)))
        src, _, _ = piece(even(e), j)
        return remote(
            src, stage.at[e, pl.ds(j, 1)], side_send.at[e, j], stage_recv.at[e, j], to, p
        )

    def near_copy(j, e=2):
        src, dst, sem = piece(even(e), j)
        return remote(src, dst, side_send.at[e, j], sem, sec(side), target(even(e)))

    def pass_copy(e, j):
        _, dst, sem = piece(even(e), j)
        return remote(
            stage.at[e, pl.ds(j, 1)], dst, pass_send.at[e, j], sem, s, target(even(e))
        )

    def own_copy(e):
        k = odd(e)
        return remote(unit(k), held(1, k), own_send.at[e], odd_recv.at[k], s, target(k))

    def own_stay(e):
        k = odd(e)
        return pltpu.make_async_copy(unit(k), held(1, k), odd_recv.at[k])

    def own_start_one(e):
        @pl.when(target(odd(e)) != p)
        def _():
            own_copy(e).start()

        @pl.when(target(odd(e)) == p)
        def _():
            own_stay(e).start()

    def own_wait():
        @pl.loop(0, 4)
        def _(e):
            @pl.when(target(odd(e)) != p)
            def _():
                own_copy(e).wait_send()

    def pass_start_one(e):
        for j in range(NB):
            side_copy(e, j).wait_recv()
            pass_copy(e, j).start()

    def from_plane(step, zero, one):
        @pl.when(side == -step * width)
        def _():
            zero(0)

        @pl.when(side == step * width)
        def _():
            one(3)
            one(1)

    def pass_start(step):
        from_plane(step, pass_start_one, pass_start_one)

    def pass_wait(step):
        def wait(e):
            for j in range(NB):
                pass_copy(e, j).wait_send()

        from_plane(step, wait, wait)

    waits = lax.rem(plane, 2) == 1

    def goes_first(e):
        return jnp.logical_not(waits) | (e == 3 * (1 - core))

    meta_wait(HALF - 2, HALF)
    pick(even(3))
    for j in range(NB):
        side_copy(3, j).start()

    meta_wait(0, HALF - 2)
    pick(even(0))
    for j in range(NB):
        side_copy(0, j).start()

    @pl.loop(0, 4)
    def _(e):
        pick(odd(e))

        @pl.when(goes_first(e))
        def _():
            own_start_one(e)

    pick(even(1))
    pick(even(2))

    fetch[1].wait()
    fetch[2].wait()
    fetch[3].wait()

    @pl.loop(0, rows)
    def _(m):
        pair = new_raw[0, m].astype(jnp.float32)
        new_own[m, 0] = jnp.concatenate([pair[0], pair[1]], axis=0)
        new_own[m, 1] = jnp.concatenate([pair[1], pair[0]], axis=0)

    new_copy.start()

    @pl.when(worker)
    def _():
        gain_copy.start()

    @pl.when(s == 0)
    def _():
        for h in range(HQ):
            hidden_f[:, h, :] = hidden[:, h * HD : (h + 1) * HD].astype(jnp.float32)

        @pl.loop(0, rows)
        def _(m):
            first[m] = hidden_f[m].astype(jnp.bfloat16)
            first_copy(m).start()

    for j in range(NB):
        side_copy(3, j).wait_send()
        side_copy(1, j).start()
        side_copy(0, j).wait_send()
        near_copy(j).start()

    lead = jnp.where((plane == 0) | (plane == PLANES - 1), 1, -1)

    @pl.when(plane == 0)
    def _():
        own_wait()

    pass_start(lead)

    @pl.when(waits)
    def _():
        pass_wait(lead)

        @pl.loop(0, 4)
        def _(e):
            @pl.when(jnp.logical_not(goes_first(e)))
            def _():
                own_start_one(e)

    def passes_left():
        @pl.when(jnp.logical_not(waits))
        def _():
            pass_wait(lead)

        pass_start(-lead)

    def relay_copy(i, section):
        return remote(x_out.at[i], x_in.at[i], x_send.at[i], x_recv.at[i], section, p)

    def home_copy(home, m, section, replica):
        return remote(
            x_out.at[home * rows + m], out_ref.at[m], out_send.at[home * rows + m], out_recv.at[m],
            section, replica,
        )

    def work(home):
        layer = sec(-side * (1 - home))
        remote(new_own, new_in.at[home], new_send, new_recv.at[home], s, p).wait_recv()

        if home == 0:
            gain_copy.wait_recv()

        @pl.loop(0, HALF)
        def _(k):
            if home == 0:
                for j in range(NB):
                    src, dst, sem = piece(k, j)
                    remote(src, dst, side_send.at[0, j], sem, s, p).wait_recv()
            else:
                remote(unit(k), held(1, k), own_send.at[0], odd_recv.at[k], s, p).wait_recv()

        def row(m):
            i = home * rows + m
            info = MID + 1 - home
            slots = [metas[info, 1, j * rows + m] for j in range(NB)]
            return layer_row(
                x_in[i], gains[home], (kv_even, kv_odd)[home], slots, metas[info, 2, m],
                new_in[home, m],
            )

        def step(ms):
            for m in ms:
                relay_copy(home * rows + m, s).wait_recv()
            results = [row(m) for m in ms]
            for m, result in zip(ms, results):
                i = home * rows + m
                x_out[i] = result

                @pl.when(layer < sections - 1)
                def _():
                    relay_copy(i, sec(1)).start()

                home_copy(home, m, layer, at(MID - 1 + home)).start()

        @pl.when(layer == 0)
        def _():
            @pl.loop(0, rows // 2)
            def _(t):
                step([2 * t, 2 * t + 1])

        @pl.when(layer > 0)
        def _():
            @pl.loop(0, rows)
            def _(m):
                step([m])

    def work_wait(home):
        layer = sec(-side * (1 - home))

        @pl.loop(0, rows)
        def _(m):
            @pl.when(layer < sections - 1)
            def _():
                relay_copy(home * rows + m, sec(1)).wait_send()

            home_copy(home, m, layer, at(MID - 1 + home)).wait_send()

    other = sec(-side)
    early = jnp.minimum(s, other) < width
    odd_first = (other > s).astype(jnp.int32)
    left_turn = jnp.where(worker & early, 2 - odd_first, 0)

    @pl.loop(0, 3)
    def _(turn):
        @pl.when(turn == left_turn)
        def _():
            passes_left()

        @pl.when(worker & (turn == 1))
        def _():
            work(0)

        @pl.when(worker & (turn == 2 - 2 * odd_first))
        def _():
            work(1)

    @pl.when(worker)
    def _():
        work_wait(0)
        work_wait(1)
        gain_copy.wait_send()

    @pl.loop(0, HALF)
    def _(k):
        meta_copy(k).wait_send()

    for j in range(NB):
        near_copy(j).wait_send()
        side_copy(1, j).wait_send()

    pass_wait(-lead)

    @pl.when(plane > 0)
    def _():
        own_wait()

    new_copy.wait_send()

    @pl.loop(0, rows)
    def _(m):
        @pl.when(s == 0)
        def _():
            first_copy(m).wait_send()

        home_copy(0, m, s, p).wait_recv()


def per_device(hidden_in, norm_gain, new_kv, parked, cache_len, block_home):
    replicas = lax.axis_size("replica")
    sections = lax.axis_size("section")
    blocks = parked[0]
    rows = block_home.shape[0]
    total = 2 * rows
    hbm = pl.BlockSpec(memory_space=pl.ANY)
    dma = pltpu.SemaphoreType.DMA
    out = pl.pallas_call(
        functools.partial(kernel, sections, replicas, rows),
        out_shape=jax.ShapeDtypeStruct((rows, HQ, HD), jnp.bfloat16),
        in_specs=[hbm] * 6,
        out_specs=hbm,
        scratch_shapes=[
            pltpu.VMEM(blocks.shape, jnp.bfloat16),
            pltpu.VMEM(blocks.shape, jnp.bfloat16),
            pltpu.VMEM((4, NB) + blocks.shape[1:], jnp.bfloat16),
            pltpu.VMEM(blocks.shape, jnp.bfloat16),
            pltpu.VMEM(blocks.shape, jnp.bfloat16),
            pltpu.SMEM((NB, rows), jnp.int32),
            pltpu.SMEM((1, rows), jnp.int32),
            pltpu.VMEM((8, 128), jnp.int32),
            pltpu.VMEM((HALF, 8, 128), jnp.int32),
            pltpu.SMEM((HALF, 8, 128), jnp.int32),
            pltpu.VMEM(hidden_in.shape, jnp.bfloat16),
            pltpu.VMEM((rows, HQ, HD), jnp.float32),
            pltpu.VMEM((rows, HQ, HD), jnp.bfloat16),
            pltpu.VMEM((total, HQ, HD), jnp.bfloat16),
            pltpu.VMEM((total, HQ, HD), jnp.bfloat16),
            pltpu.VMEM(new_kv.shape, jnp.bfloat16),
            pltpu.VMEM((rows, 2, 2 * KVH, HD), jnp.float32),
            pltpu.VMEM((2, rows, 2, 2 * KVH, HD), jnp.float32),
            pltpu.VMEM((2, HQ, HD), jnp.float32),
            dma((7,)),
            dma((HALF,)), dma((HALF,)), dma((4, NB)), dma((4, NB)), dma((4, NB)), dma((4,)),
            dma((HALF, NB)), dma((HALF,)),
            dma((total,)), dma((total,)), dma((total,)), dma((rows,)),
            dma((rows,)), dma, dma((2,)), dma, dma,
        ],
        compiler_params=pltpu.CompilerParams(
            collective_id=0, has_side_effects=True, vmem_limit_bytes=56 * 1024 * 1024
        ),
    )(block_home.T, cache_len.reshape(1, rows), hidden_in, new_kv, norm_gain.reshape(HQ, HD), blocks)
    return out.reshape(1, rows, HQ * HD)


def solution(mesh):
    return jax.shard_map(
        per_device,
        mesh=mesh,
        in_specs=(
            P("replica", None),
            P("section", None),
            P("section", "replica", None, None, None),
            P("section", "replica", None, None, None, None),
            P("replica"),
            P("replica", None),
        ),
        out_specs=P("section", "replica", None),
        check_vma=False,
    )
```
